512 devices in a mesh: row: 32 (over x_hi, y, core), col: 16 (over z, x_lo).
Axes of the slice: x: 4 (x_hi: 2, x_lo: 2; x = x_hi * 2 + x_lo), y: 8, z: 8, core: 2. Of those that a mesh axis runs over, the one named last changes fastest.
Arguments:
- amplitudes: float32 [8, 8192, 6144], P(None, 'row', 'col'), may hold values from -6 to 6
- integrals: float32 [8, 512, 6144], P(None, 'row', 'col'), may hold values from -0.078125 to 0.078125
- residual_in: float32 [8, 8192, 512], P(None, ('row', 'col')), may hold values from -3 to 3
- cd_count: int32 [8], replicated, may hold values from 3072 to 6144, as said below
Outputs:
- residual: float32 [8, 8192, 512], P(None, ('row', 'col'))
The draws below stay inside these ranges and needn't reach their ends.
Inputs may be any that keep to these rules, and one draw needn't show every extreme that they name: Live contracted pairs of an irrep are the first cd_count of its 6144 slots; some irrep has all 6144 slots live in every draw.
All inputs are finite; a program needn't handle non-finite values.
Results may differ from the reference program's by a relative error of at most 0.0003.
Values sent between devices are 32-bit elements; how exact they have to be, the bound alone decides.
No kernel may reach another device: no remote copies, remote signals or barrier semaphores. Data moves between devices by JAX's collectives and lax.ppermute only.
A program may use at most 64 MiB of HBM per device.

```python
import jax
import jax.numpy as jnp
from jax import lax

IRREPS = 8
IJ_H = 8192
AB_H = 512
CD_H = 6144


def draw_cd_count(key, part):
    key = jax.random.fold_in(key, 7)
    first, second = jax.random.split(key)
    counts = jax.random.randint(first, (IRREPS,), CD_H // 2, CD_H + 1)
    fullest = jax.random.randint(second, (), 0, IRREPS)
    return jnp.where(jnp.arange(IRREPS) == fullest, CD_H, counts).astype(jnp.int32)


def shard_levels(key, shape, cuts, low, high):
    loudness, own = 1.0, jax.random.fold_in(key, 6)
    for dim, shards_of in cuts:
        heights = jnp.exp(jax.random.uniform(jax.random.fold_in(own, dim), (shards_of,), jnp.float32, low / len(cuts), high / len(cuts)))
        loudness = loudness * jnp.repeat(heights, shape[dim] // shards_of).reshape([-1 if axis == dim else 1 for axis in range(len(shape))])
    return loudness


def noise(own_key, shape, deviation, bound, shards=(), kind=jnp.bfloat16):
    array = deviation * jax.random.normal(own_key, shape, jnp.float32)
    if shards:
        array = array * shard_levels(own_key, shape, shards, -0.22, 0.18)
    return jnp.clip(array, -bound, bound).astype(kind)


def setup_inputs(seed: int = 0) -> dict:
    keys = jax.random.split(jax.random.key(seed), 5)
    return {
        "amplitudes": noise(keys[0], (IRREPS, IJ_H, CD_H), 1.0, 6.0, ((1, 32), (2, 16)), jnp.float32),
        "integrals": noise(keys[1], (IRREPS, AB_H, CD_H), CD_H ** -0.5, 0.078125, ((1, 32), (2, 16)), jnp.float32),
        "residual_in": noise(keys[2], (IRREPS, IJ_H, AB_H), 0.5, 3.0, ((1, 512),), jnp.float32),
        "cd_count": draw_cd_count(jax.random.fold_in(keys[4], 71), 0),
    }


def one_irrep(packed):
    block, weights, count = packed
    slots = lax.broadcasted_iota(jnp.int32, (1, block.shape[1]), 1)
    live = jnp.where(slots < count, block, jnp.zeros_like(block))
    return jnp.dot(live, weights.T, precision=lax.Precision.HIGHEST)


def reference(amplitudes, integrals, residual_in, cd_count):
    ladder = lax.map(one_irrep, (amplitudes, integrals, cd_count.astype(jnp.int32)))
    return residual_in + ladder
```

```python
import jax
import jax.numpy as jnp
from jax import lax
from jax.sharding import Mesh, PartitionSpec as P

LINE = ("xh", "core", "xl")


def body(amplitudes, integrals, residual_in, cd_count):
    width = amplitudes.shape[2]
    v = lax.all_to_all(integrals, LINE, 0, 0, tiled=True)
    v = lax.all_gather(v, "y", axis=0)
    t = lax.all_to_all(amplitudes, LINE, 0, 0, tiled=True)

    count = cd_count[lax.axis_index(LINE)]
    v = v.reshape(8, 2, 2, 2, 16, width)
    t = t.reshape(2, 2, 2, 256, width)
    slots = lax.broadcasted_iota(jnp.int32, (2, 1, width), 0) * width + lax.broadcasted_iota(jnp.int32, (2, 1, width), 2)
    slots = slots + lax.axis_index("z") * (2 * width)
    v = v.transpose(3, 1, 0, 2, 4, 5).reshape(2, 512, width)
    v = jnp.where(slots < count, v, jnp.zeros_like(v))
    t = t.transpose(2, 0, 1, 3, 4).reshape(2, 1024, width)
    sums = jnp.einsum("xic,xac->ia", t, v, precision=lax.Precision.HIGH)
    sums = sums.reshape(2, 2, 8, 2, 16, 512).transpose(2, 0, 1, 3, 4, 5).reshape(8, 8, 16, 512)
    mine = lax.psum_scatter(sums, "z", scatter_dimension=0)
    ladder = lax.all_to_all(mine, LINE, 0, 0, tiled=True)
    return residual_in + ladder


def solution(mesh):
    mesh = Mesh(mesh.devices.reshape(2, 8, 2, 8, 2), ("xh", "y", "core", "z", "xl"))
    row, col = ("xh", "y", "core"), ("z", "xl")
    in_specs = (P(None, row, col), P(None, row, col), P(None, row + col, None), P())
    return jax.shard_map(body, mesh=mesh, in_specs=in_specs, out_specs=P(None, row + col, None), check_vma=False)
```

```python
import functools

import jax
import jax.numpy as jnp
from jax import lax
from jax.experimental import pallas as pl
from jax.experimental.pallas import tpu as pltpu
from jax.sharding import Mesh, PartitionSpec as P

LINE = ("xh", "core", "xl")
N_Z = N_Y = 8
N_LINE = 8
EARLY = (3, 4, 5)
LATE = (2, 6, 1, 7, 0)


def shift(x, axis, by, size):
    return lax.ppermute(x, axis, [(i, (i + by) % size) for i in range(size)])


def split(x):
    high = x.astype(jnp.bfloat16)
    return high, (x - high.astype(jnp.float32)).astype(jnp.bfloat16)


def product(t_high, t_low, v_high, v_low):
    dot = functools.partial(
        lax.dot_general, dimension_numbers=(((1,), (1,)), ((), ())), preferred_element_type=jnp.float32
    )
    return dot(t_high, v_high) + (dot(t_low, v_high) + dot(t_high, v_low))


def fill_t(t_refs, th, tl):
    rows, width = t_refs[0].shape[1:]
    for k, t_ref in enumerate(t_refs):
        for g in range(N_LINE):
            part, x = divmod(g, 2)
            high, low = split(t_ref[g])
            at = (slice((4 * k + part) * rows, (4 * k + part + 1) * rows), slice(x * width, (x + 1) * width))
            th[at] = high
            tl[at] = low


def early_kernel(meta, v_ref, t3, t4, t5, p3, p4a, p4b, p5, vh, vl, th, tl):
    rows, width = v_ref.shape[2:]
    slots = lax.broadcasted_iota(jnp.int32, (rows, width), 1)
    for y in range(N_Y):
        for g in range(N_LINE):
            part, x = divmod(g, 2)
            xh, core = divmod(part, 2)
            high, low = split(jnp.where(slots + x * width < meta[16], v_ref[y, g], 0.0))
            at = (slice(((xh * N_Y + y) * 2 + core) * rows, ((xh * N_Y + y) * 2 + core + 1) * rows), slice(x * width, (x + 1) * width))
            vh[at] = high
            vl[at] = low
    fill_t((t3, t4, t5), th, tl)
    sums = product(th[...], tl[...], vh[...], vl[...])
    chunk = p3.shape[0]
    p3[...] = sums[:chunk]
    p4a[...] = sums[chunk : chunk + chunk // 2]
    p4b[...] = sums[chunk + chunk // 2 : 2 * chunk]
    p5[...] = sums[2 * chunk :]


def late_kernel(meta, vh, vl, *refs):
    n = len(LATE)
    t_refs, p_refs, (th, tl) = refs[:n], refs[n : 2 * n], refs[2 * n :]
    fill_t(t_refs, th, tl)
    sums = product(th[...], tl[...], vh[...], vl[...])
    chunk = p_refs[0].shape[0]
    for k, p_ref in enumerate(p_refs):
        p_ref[...] = sums[k * chunk : (k + 1) * chunk]


def relay_kernel(first, own, came, half, out):
    out[...] = own[...] + came[...]
    rows = half.shape[0]
    at = slice(0, rows) if first else slice(rows, 2 * rows)
    out[at] += half[...]


def call(kernel, meta, arrays, specs, outs, scratch, flops):
    whole = lambda shape: pl.BlockSpec(shape, lambda i, m, n=len(shape): (0,) * n)
    return pl.pallas_call(
        kernel,
        out_shape=[jax.ShapeDtypeStruct(*o) for o in outs],
        grid_spec=pltpu.PrefetchScalarGridSpec(
            num_scalar_prefetch=1,
            grid=(1,),
            in_specs=[whole(a.shape) if s is None else s for a, s in zip(arrays, specs)],
            out_specs=[whole(o[0]) for o in outs],
            scratch_shapes=scratch,
        ),
        compiler_params=pltpu.CompilerParams(vmem_limit_bytes=32 << 20),
        cost_estimate=pl.CostEstimate(flops=flops, bytes_accessed=4 << 20, transcendentals=0),
    )(meta, *arrays)


def relay(first, own, came, half):
    return pl.pallas_call(
        functools.partial(relay_kernel, first),
        out_shape=jax.ShapeDtypeStruct(own.shape, own.dtype),
        cost_estimate=pl.CostEstimate(flops=own.size, bytes_accessed=own.size * 12, transcendentals=0),
    )(own, came, half)


def body(amplitudes, integrals, residual_in, cd_count):
    width = amplitudes.shape[2]
    y, z = lax.axis_index("y"), lax.axis_index("z")
    steps = jnp.arange(8, dtype=jnp.int32)
    live = cd_count[lax.axis_index(LINE)] - z * (2 * width)
    meta = jnp.concatenate([(z + steps) % N_Z, (y + steps) % N_Y, live[None]]).astype(jnp.int32)

    v = lax.all_to_all(integrals, LINE, 0, 0, tiled=True)
    v = lax.all_gather(v, "y", axis=0)
    t = lax.all_to_all(amplitudes, LINE, 0, 0, tiled=True)

    rows, outer = 32, 512
    chunk = 4 * rows
    f32, bf16 = jnp.float32, jnp.bfloat16
    t_spec = lambda k: pl.BlockSpec((N_LINE, rows, width), lambda i, m, k=k: (0, m[k], 0))
    t_halves = lambda n: [pltpu.VMEM((n * chunk, 2 * width), bf16)] * 2
    flops = 6 * chunk * 2 * width * outer
    p3, p4a, p4b, p5, vh, vl = call(
        early_kernel, meta, [v, t, t, t], [None] + [t_spec(k) for k in EARLY],
        [((chunk, outer), f32), ((chunk // 2, outer), f32), ((chunk // 2, outer), f32), ((chunk, outer), f32)]
        + [((outer, 2 * width), bf16)] * 2,
        t_halves(len(EARLY)), flops * len(EARLY),
    )
    r3 = shift(p3, "z", 1, N_Z)
    r5 = shift(p5, "z", -1, N_Z)
    r4a = shift(p4a, "z", 2, N_Z)
    r4b = shift(p4b, "z", -2, N_Z)
    p2, p6, p1, p7, p0 = call(
        late_kernel, meta, [vh, vl] + [t] * len(LATE), [None, None] + [t_spec(k) for k in LATE],
        [((chunk, outer), f32)] * len(LATE), t_halves(len(LATE)), flops * len(LATE),
    )
    d1 = shift(p1, "z", 1, N_Z)
    d7 = shift(p7, "z", -1, N_Z)
    d2 = shift(relay(True, p2, r3, r4a), "z", 2, N_Z)
    d6 = shift(relay(False, p6, r5, r4b), "z", -2, N_Z)
    mine = p0 + d1 + d7 + d2 + d6
    ladder = lax.all_to_all(mine.reshape(N_LINE, 16, outer), LINE, 0, 0, tiled=True)
    return residual_in + ladder


def solution(mesh):
    mesh = Mesh(mesh.devices.reshape(2, 8, 2, 8, 2), ("xh", "y", "core", "z", "xl"))
    row, col = ("xh", "y", "core"), ("z", "xl")
    in_specs = (P(None, row, col), P(None, row, col), P(None, row + col, None), P())
    return jax.shard_map(body, mesh=mesh, in_specs=in_specs, out_specs=P(None, row + col, None), check_vma=False)
```

```python
import functools

import jax
import jax.numpy as jnp
from jax import lax
from jax.experimental import pallas as pl
from jax.experimental.pallas import tpu as pltpu
from jax.sharding import Mesh, PartitionSpec as P

LINE = ("xh", "core", "xl")
N_Y = N_Z = N_LINE = 8
ROWS = 16
OUTER = 512
STEPS = 2


def split(x):
    high = x.astype(jnp.bfloat16)
    return high, (x - high.astype(jnp.float32)).astype(jnp.bfloat16)


def sums_kernel(live, v0, v1, t_ref, out, th, tl, vh, vl):
    width = t_ref.shape[2]

    @pl.when(pl.program_id(0) == 0)
    def _():
        slots = lax.broadcasted_iota(jnp.int32, (ROWS, width), 1)
        for xh, v_ref in enumerate((v0, v1)):
            for core in range(2):
                for y in range(N_Y):
                    for x in range(2):
                        block = v_ref[core, (y * 2 + x) * ROWS : (y * 2 + x + 1) * ROWS]
                        high, low = split(jnp.where(slots + x * width < live[0], block, 0.0))
                        row = ((xh * N_Y + y) * 2 + core) * ROWS
                        at = (slice(row, row + ROWS), slice(x * width, (x + 1) * width))
                        vh[at] = high
                        vl[at] = low

    for z in range(N_Z // STEPS):
        for g in range(N_LINE):
            part, x = divmod(g, 2)
            high, low = split(t_ref[g, z * 32 : (z + 1) * 32])
            at = (slice((z * 4 + part) * 32, (z * 4 + part + 1) * 32), slice(x * width, (x + 1) * width))
            th[at] = high
            tl[at] = low
    dot = functools.partial(
        lax.dot_general, dimension_numbers=(((1,), (1,)), ((), ())), preferred_element_type=jnp.float32
    )
    out[...] = dot(th[...], vh[...]) + (dot(tl[...], vh[...]) + dot(th[...], vl[...]))


def partial_sums(live, v0, v1, t):
    rows, width = t.shape[1] // STEPS, t.shape[2]
    total = 4 * t.shape[1]
    half = total // STEPS
    v_spec = pl.BlockSpec(v0.shape, lambda i, m: (0, 0, 0))
    return pl.pallas_call(
        sums_kernel,
        out_shape=jax.ShapeDtypeStruct((total, OUTER), jnp.float32),
        grid_spec=pltpu.PrefetchScalarGridSpec(
            num_scalar_prefetch=1,
            grid=(STEPS,),
            in_specs=[v_spec, v_spec, pl.BlockSpec((N_LINE, rows, width), lambda i, m: (0, i, 0))],
            out_specs=pl.BlockSpec((half, OUTER), lambda i, m: (i, 0)),
            scratch_shapes=[pltpu.VMEM((half, 2 * width), jnp.bfloat16)] * 2
            + [pltpu.VMEM((OUTER, 2 * width), jnp.bfloat16)] * 2,
        ),
        compiler_params=pltpu.CompilerParams(vmem_limit_bytes=32 << 20),
        cost_estimate=pl.CostEstimate(flops=12 * total * width * OUTER, bytes_accessed=8 << 20, transcendentals=0),
    )(live, v0, v1, t)


def body(amplitudes, integrals, residual_in, cd_count):
    width = amplitudes.shape[2]
    live = cd_count[lax.axis_index(LINE)] - lax.axis_index("z") * (2 * width)

    v = lax.all_to_all(integrals, LINE, 0, 0, tiled=True)
    t = lax.all_to_all(amplitudes, LINE, 0, 0, tiled=True)
    v = v.reshape(2, 2, 2 * ROWS, width)
    v0, v1 = (lax.all_gather(v[xh], "y", axis=1, tiled=True) for xh in range(2))

    sums = partial_sums(live[None].astype(jnp.int32), v0, v1, t)
    mine = lax.psum_scatter(sums.reshape(N_Z, N_LINE * ROWS, OUTER), "z", scatter_dimension=0)
    ladder = lax.all_to_all(mine.reshape(N_LINE, ROWS, OUTER), LINE, 0, 0, tiled=True)
    return residual_in + ladder


def solution(mesh):
    mesh = Mesh(mesh.devices.reshape(2, 8, 2, 8, 2), ("xh", "y", "core", "z", "xl"))
    row, col = ("xh", "y", "core"), ("z", "xl")
    in_specs = (P(None, row, col), P(None, row, col), P(None, row + col, None), P())
    return jax.shard_map(body, mesh=mesh, in_specs=in_specs, out_specs=P(None, row + col, None), check_vma=False)
```

```python
import functools

import jax
import jax.numpy as jnp
from jax import lax
from jax.experimental import pallas as pl
from jax.experimental.pallas import tpu as pltpu
from jax.sharding import Mesh, PartitionSpec as P

GROUP = ("core", "z0", "xl")
N_Y, N_ZQ, N_GROUP = 8, 4, 8
ROWS = 16
OUTER = 512
STEPS = 2


def split(x):
    high = x.astype(jnp.bfloat16)
    return high, (x - high.astype(jnp.float32)).astype(jnp.bfloat16)


def sums_kernel(live, v_ref, t_ref, out, th, tl, vh, vl):
    width = t_ref.shape[2]

    @pl.when(pl.program_id(0) == 0)
    def _():
        slots = lax.broadcasted_iota(jnp.int32, (ROWS, width), 1)
        for y in range(N_Y):
            for xh in range(2):
                for g in range(N_GROUP):
                    core, c = divmod(g, 4)
                    block = jnp.where(slots + c * width < live[0], v_ref[y, xh * N_GROUP + g], 0.0)
                    high, low = split(block)
                    row = ((xh * N_Y + y) * 2 + core) * ROWS
                    at = (slice(row, row + ROWS), slice(c * width, (c + 1) * width))
                    vh[at] = high
                    vl[at] = low

    for zq in range(N_ZQ // STEPS):
        for g in range(N_GROUP):
            core, c = divmod(g, 4)
            high, low = split(t_ref[g, zq * 64 : (zq + 1) * 64])
            at = (slice((zq * 2 + core) * 64, (zq * 2 + core + 1) * 64), slice(c * width, (c + 1) * width))
            th[at] = high
            tl[at] = low
    dot = functools.partial(
        lax.dot_general, dimension_numbers=(((1,), (1,)), ((), ())), preferred_element_type=jnp.float32
    )
    out[...] = dot(th[...], vh[...]) + (dot(tl[...], vh[...]) + dot(th[...], vl[...]))


def partial_sums(live, v, t):
    rows, width = t.shape[1] // STEPS, t.shape[2]
    total = 2 * t.shape[1]
    part = total // STEPS
    return pl.pallas_call(
        sums_kernel,
        out_shape=jax.ShapeDtypeStruct((total, OUTER), jnp.float32),
        grid_spec=pltpu.PrefetchScalarGridSpec(
            num_scalar_prefetch=1,
            grid=(STEPS,),
            in_specs=[
                pl.BlockSpec(v.shape, lambda i, m: (0, 0, 0, 0)),
                pl.BlockSpec((N_GROUP, rows, width), lambda i, m: (0, i, 0)),
            ],
            out_specs=pl.BlockSpec((part, OUTER), lambda i, m: (i, 0)),
            scratch_shapes=[pltpu.VMEM((part, 4 * width), jnp.bfloat16)] * 2
            + [pltpu.VMEM((OUTER, 4 * width), jnp.bfloat16)] * 2,
        ),
        compiler_params=pltpu.CompilerParams(vmem_limit_bytes=56 << 20),
        cost_estimate=pl.CostEstimate(flops=24 * total * width * OUTER, bytes_accessed=8 << 20, transcendentals=0),
    )(live, v, t)


def body(amplitudes, integrals, residual_in, cd_count):
    width = amplitudes.shape[2]
    live = cd_count[lax.axis_index(GROUP)] - lax.axis_index("zq") * (4 * width)

    v = lax.all_to_all(jnp.concatenate([integrals, integrals]), ("xh",) + GROUP, 0, 0, tiled=True)
    v = lax.all_gather(v, "y", axis=0)
    t = lax.all_to_all(amplitudes, GROUP, 0, 0, tiled=True)

    sums = partial_sums(live[None].astype(jnp.int32), v, t)
    mine = lax.psum_scatter(sums.reshape(N_ZQ, N_GROUP * ROWS, OUTER), "zq", scatter_dimension=0)
    ladder = lax.all_to_all(mine.reshape(N_GROUP, ROWS, OUTER), GROUP, 0, 0, tiled=True)
    return residual_in + ladder


def solution(mesh):
    mesh = Mesh(mesh.devices.reshape(2, 8, 2, 4, 2, 2), ("xh", "y", "core", "zq", "z0", "xl"))
    row, col = ("xh", "y", "core"), ("zq", "z0", "xl")
    in_specs = (P(None, row, col), P(None, row, col), P(None, row + col, None), P())
    return jax.shard_map(body, mesh=mesh, in_specs=in_specs, out_specs=P(None, row + col, None), check_vma=False)
```

```python
import functools

import jax
import jax.numpy as jnp
from jax import lax
from jax.experimental import pallas as pl
from jax.experimental.pallas import tpu as pltpu
from jax.sharding import Mesh, PartitionSpec as P

GROUP = ("core", "z0", "xl")
N_Y, N_ZQ, N_GROUP = 8, 4, 8
ROWS = 16
OUTER = 512


def split(x):
    high = x.astype(jnp.bfloat16)
    return high, (x - high.astype(jnp.float32)).astype(jnp.bfloat16)


def pair_kernel(t_ref, th, tl):
    rows, width = t_ref.shape[1:]
    for c in range(4):
        th[:, c * width : (c + 1) * width], tl[:, c * width : (c + 1) * width] = split(t_ref[c])


def pairs(t):
    rows, width = t.shape[1] // N_ZQ, t.shape[2]
    total = 2 * t.shape[1]
    out_spec = pl.BlockSpec((rows, 4 * width), lambda zq, core: (2 * zq + core, 0))
    return pl.pallas_call(
        pair_kernel,
        out_shape=[jax.ShapeDtypeStruct((total, 4 * width), jnp.bfloat16)] * 2,
        grid=(N_ZQ, 2),
        in_specs=[pl.BlockSpec((4, rows, width), lambda zq, core: (core, zq, 0))],
        out_specs=[out_spec] * 2,
        compiler_params=pltpu.CompilerParams(vmem_limit_bytes=60 << 20),
        cost_estimate=pl.CostEstimate(flops=3 * t.size, bytes_accessed=8 * t.size, transcendentals=0),
    )(t)


def sums_kernel(live, v_ref, th, tl, out, vh, vl):
    width = v_ref.shape[3]
    slots = lax.broadcasted_iota(jnp.int32, (ROWS, width), 1)
    for y in range(N_Y):
        for xh in range(2):
            for g in range(N_GROUP):
                core, c = divmod(g, 4)
                block = jnp.where(slots + c * width < live[0], v_ref[y, xh * N_GROUP + g], 0.0)
                high, low = split(block)
                row = ((xh * N_Y + y) * 2 + core) * ROWS
                at = (slice(row, row + ROWS), slice(c * width, (c + 1) * width))
                vh[at] = high
                vl[at] = low
    dot = functools.partial(
        lax.dot_general, dimension_numbers=(((1,), (1,)), ((), ())), preferred_element_type=jnp.float32
    )
    out[...] = dot(th[...], vh[...]) + (dot(tl[...], vh[...]) + dot(th[...], vl[...]))


def partial_sums(live, v, th, tl):
    whole = lambda a: pl.BlockSpec(a.shape, lambda i, m: (0,) * a.ndim)
    out = jax.ShapeDtypeStruct((th.shape[0], OUTER), jnp.float32)
    return pl.pallas_call(
        sums_kernel,
        out_shape=out,
        grid_spec=pltpu.PrefetchScalarGridSpec(
            num_scalar_prefetch=1,
            grid=(1,),
            in_specs=[whole(v), whole(th), whole(tl)],
            out_specs=whole(out),
            scratch_shapes=[pltpu.VMEM((OUTER, th.shape[1]), jnp.bfloat16)] * 2,
        ),
        compiler_params=pltpu.CompilerParams(vmem_limit_bytes=60 << 20),
        cost_estimate=pl.CostEstimate(flops=6 * th.size * OUTER, bytes_accessed=8 << 20, transcendentals=0),
    )(live, v, th, tl)


def body(amplitudes, integrals, residual_in, cd_count):
    width = amplitudes.shape[2]
    live = cd_count[lax.axis_index(GROUP)] - lax.axis_index("zq") * (4 * width)

    v = lax.all_to_all(jnp.concatenate([integrals, integrals]), ("xh",) + GROUP, 0, 0, tiled=True)
    v = lax.all_gather(v, "y", axis=0)
    th, tl = pairs(lax.all_to_all(amplitudes, GROUP, 0, 0, tiled=True))

    sums = partial_sums(live[None].astype(jnp.int32), v, th, tl)
    parts = lax.all_to_all(sums.reshape(N_ZQ * N_GROUP, ROWS, OUTER), ("zq",) + GROUP, 0, 0, tiled=True)
    return residual_in + jnp.sum(parts.reshape(N_ZQ, N_GROUP, ROWS, OUTER), axis=0)


def solution(mesh):
    mesh = Mesh(mesh.devices.reshape(2, 8, 2, 4, 2, 2), ("xh", "y", "core", "zq", "z0", "xl"))
    row, col = ("xh", "y", "core"), ("zq", "z0", "xl")
    in_specs = (P(None, row, col), P(None, row, col), P(None, row + col, None), P())
    return jax.shard_map(body, mesh=mesh, in_specs=in_specs, out_specs=P(None, row + col, None), check_vma=False)
```

```python
import functools

import jax
import jax.numpy as jnp
from jax import lax
from jax.experimental import pallas as pl
from jax.experimental.pallas import tpu as pltpu
from jax.sharding import Mesh, PartitionSpec as P

GROUP = ("xh", "z0", "xl")
N_Y, N_ZQ, N_GROUP = 8, 4, 8
ROWS = 16
OUTER = 512
HALF = OUTER // 2
STEPS = 2

DOT = functools.partial(
    lax.dot_general, dimension_numbers=(((1,), (1,)), ((), ())), preferred_element_type=jnp.float32
)


def split(x):
    high = x.astype(jnp.bfloat16)
    return high, (x - high.astype(jnp.float32)).astype(jnp.bfloat16)


def pair_kernel(live, t_ref, th, tl):
    rows, width = t_ref.shape[1:]
    slots = lax.broadcasted_iota(jnp.int32, (rows, width), 1)
    for g in range(N_GROUP):
        xh, c = divmod(g, 4)
        at = (slice(xh * rows, (xh + 1) * rows), slice(c * width, (c + 1) * width))
        th[at], tl[at] = split(jnp.where(slots + c * width < live[0], t_ref[g], 0.0))


def pairs(live, t):
    rows, width = t.shape[1] // N_ZQ, t.shape[2]
    total = 2 * t.shape[1]
    return pl.pallas_call(
        pair_kernel,
        out_shape=[pltpu.HBM((total, 4 * width), jnp.bfloat16)] * 2,
        grid_spec=pltpu.PrefetchScalarGridSpec(
            num_scalar_prefetch=1,
            grid=(N_ZQ,),
            in_specs=[pl.BlockSpec((N_GROUP, rows, width), lambda zq, m: (0, zq, 0))],
            out_specs=[pl.BlockSpec((2 * rows, 4 * width), lambda zq, m: (zq, 0))] * 2,
        ),
        compiler_params=pltpu.CompilerParams(vmem_limit_bytes=16 << 20),
        cost_estimate=pl.CostEstimate(flops=3 * t.size, bytes_accessed=8 * t.size, transcendentals=0),
    )(live, t)


def sums_kernel(core, v_ref, th, tl, *rest):
    out, vh, vl = rest[-3:]
    width = v_ref.shape[4]
    for c in range(v_ref.shape[2]):
        for y in range(N_Y):
            for xh in range(2):
                row = (xh * N_Y + y) * ROWS
                at = (slice(row, row + ROWS), slice(c * width, (c + 1) * width))
                vh[at], vl[at] = split(v_ref[y, xh, c])
    sums = DOT(th[...], vh[...]) + (DOT(tl[...], vh[...]) + DOT(th[...], vl[...]))

    @pl.when(pl.program_id(0) == 0)
    def _():
        out[...] = sums

    @pl.when(pl.program_id(0) > 0)
    def _():
        out[...] += sums


def partial_sums(core, v, th, tl, into=None):
    width = v.shape[3]
    depth = 4 // STEPS
    v = v.reshape(N_Y, 2, 4, ROWS, width)
    total = th.shape[0]
    t_spec = pl.BlockSpec((total, depth * width), lambda k, m: (0, k))
    arrays = [core, v, th, tl] + ([] if into is None else [into])
    return pl.pallas_call(
        sums_kernel,
        out_shape=jax.ShapeDtypeStruct((total, OUTER), jnp.float32),
        grid_spec=pltpu.PrefetchScalarGridSpec(
            num_scalar_prefetch=1,
            grid=(STEPS,),
            in_specs=[pl.BlockSpec((N_Y, 2, depth, ROWS, width), lambda k, m: (0, 0, k, 0, 0)), t_spec, t_spec]
            + [pl.BlockSpec(memory_space=pl.ANY)] * (len(arrays) - 4),
            out_specs=pl.BlockSpec((total, HALF), lambda k, m: (0, m[0])),
            scratch_shapes=[pltpu.VMEM((HALF, depth * width), jnp.bfloat16)] * 2,
        ),
        input_output_aliases={} if into is None else {4: 0},
        compiler_params=pltpu.CompilerParams(vmem_limit_bytes=60 << 20),
        cost_estimate=pl.CostEstimate(flops=6 * th.size * HALF, bytes_accessed=8 << 20, transcendentals=0),
    )(*arrays)


def finish_kernel(parts, residual, out):
    ladder = (parts[0] + parts[1]) + (parts[2] + parts[3])
    to = lax.broadcasted_iota(jnp.int32, (OUTER, OUTER), 0)
    source = lax.broadcasted_iota(jnp.int32, (OUTER, OUTER), 1)
    wanted = ((to >> 4) & 1) * HALF + (to >> 5) * ROWS + (to & (ROWS - 1))
    order = jnp.where(source == wanted, 1.0, 0.0).astype(jnp.bfloat16)
    first, _ = split(ladder)
    rest = ladder - first.astype(jnp.float32)
    second, third = split(rest)
    out[...] = residual[...] + (DOT(first, order) + (DOT(second, order) + DOT(third, order)))


def finish(parts, residual):
    shape = residual.shape
    parts = parts.reshape(N_ZQ, N_GROUP * ROWS, OUTER)
    residual = residual.reshape(N_GROUP * ROWS, OUTER)
    out = pl.pallas_call(
        finish_kernel,
        out_shape=jax.ShapeDtypeStruct(residual.shape, residual.dtype),
        compiler_params=pltpu.CompilerParams(vmem_limit_bytes=32 << 20),
        cost_estimate=pl.CostEstimate(flops=6 * residual.size * OUTER, bytes_accessed=24 * residual.size, transcendentals=0),
    )(parts, residual)
    return out.reshape(shape)


def body(amplitudes, integrals, residual_in, cd_count):
    width = amplitudes.shape[2]
    live = cd_count[lax.axis_index(GROUP)] - lax.axis_index("zq") * (4 * width)
    core = lax.axis_index("core").astype(jnp.int32)

    v = lax.all_to_all(integrals, GROUP, 0, 0, tiled=True)
    v = lax.all_gather(v, "y", axis=0)
    t = lax.all_to_all(amplitudes, GROUP, 0, 0, tiled=True)
    th, tl = pairs(live[None].astype(jnp.int32), t)
    v, th, tl = lax.optimization_barrier((v, th, tl))
    other = lax.ppermute(v, "core", [(0, 1), (1, 0)])

    sums = partial_sums(core[None], v, th, tl)
    sums = partial_sums(1 - core[None], other, th, tl, sums)
    parts = lax.all_to_all(sums.reshape(N_ZQ * N_GROUP, ROWS, OUTER), ("zq",) + GROUP, 0, 0, tiled=True)
    return finish(parts, residual_in)


def solution(mesh):
    mesh = Mesh(mesh.devices.reshape(2, 8, 2, 4, 2, 2), ("xh", "y", "core", "zq", "z0", "xl"))
    row, col = ("xh", "y", "core"), ("zq", "z0", "xl")
    in_specs = (P(None, row, col), P(None, row, col), P(None, row + col, None), P())
    return jax.shard_map(body, mesh=mesh, in_specs=in_specs, out_specs=P(None, row + col, None), check_vma=False)
```

```python
import functools

import jax
import jax.numpy as jnp
from jax import lax
from jax.experimental import pallas as pl
from jax.experimental.pallas import tpu as pltpu
from jax.sharding import Mesh, PartitionSpec as P

GROUP = ("core", "z0", "xl")
N_Y, N_ZQ, N_GROUP = 8, 4, 8
ROWS = 16
OUTER = 512
STEPS = 2


def split(x):
    high = x.astype(jnp.bfloat16)
    return high, (x - high.astype(jnp.float32)).astype(jnp.bfloat16)


def pair_kernel(live, t_ref, th, tl):
    rows, width = t_ref.shape[1:]
    slots = lax.broadcasted_iota(jnp.int32, (rows, width), 1)
    for g in range(N_GROUP):
        core, c = divmod(g, 4)
        at = (slice(core * rows, (core + 1) * rows), slice(c * width, (c + 1) * width))
        th[at], tl[at] = split(jnp.where(slots + c * width < live[0], t_ref[g], 0.0))


def pairs(live, t):
    rows, width = t.shape[1] // N_ZQ, t.shape[2]
    total = 2 * t.shape[1]
    return pl.pallas_call(
        pair_kernel,
        out_shape=[pltpu.HBM((total, 4 * width), jnp.bfloat16)] * 2,
        grid_spec=pltpu.PrefetchScalarGridSpec(
            num_scalar_prefetch=1,
            grid=(N_ZQ,),
            in_specs=[pl.BlockSpec((N_GROUP, rows, width), lambda zq, m: (0, zq, 0))],
            out_specs=[pl.BlockSpec((2 * rows, 4 * width), lambda zq, m: (zq, 0))] * 2,
        ),
        compiler_params=pltpu.CompilerParams(vmem_limit_bytes=16 << 20),
        cost_estimate=pl.CostEstimate(flops=3 * t.size, bytes_accessed=8 * t.size, transcendentals=0),
    )(live, t)


NEAR = ((0, (0, 1)), (-1, (0, 1)), (1, (0, 1)), (-2, (0, 1)), (2, (0, 1)), (-3, (0, 1)), (3, (0, 1)), (4, (0,)), (4, (1,)))


def sums_kernel(ys, v_ref, *rest):
    near_refs, (th, tl, out, vh, vl) = rest[: len(NEAR)], rest[len(NEAR) :]
    depth, width = v_ref.shape[2], v_ref.shape[4]
    for c in range(depth):
        columns = slice(c * width, (c + 1) * width)
        for y in range(N_Y):
            for core in range(2):
                rows = slice((y * 2 + core) * ROWS, (y * 2 + core + 1) * ROWS)
                vh[rows, columns], vl[rows, columns] = split(v_ref[y, core, c])
        for i, (near_ref, (_, cores)) in enumerate(zip(near_refs, NEAR)):
            for j, core in enumerate(cores):
                start = pl.multiple_of(OUTER // 2 + ys[i] * (2 * ROWS) + core * ROWS, ROWS)
                rows = pl.ds(start, ROWS)
                vh[rows, columns], vl[rows, columns] = split(near_ref[j, c])
    dot = functools.partial(
        lax.dot_general, dimension_numbers=(((1,), (1,)), ((), ())), preferred_element_type=jnp.float32
    )
    sums = dot(th[...], vh[...]) + (dot(tl[...], vh[...]) + dot(th[...], vl[...]))

    @pl.when(pl.program_id(0) == 0)
    def _():
        out[...] = sums

    @pl.when(pl.program_id(0) > 0)
    def _():
        out[...] += sums


def partial_sums(ys, v, near, th, tl):
    width = v.shape[3]
    depth = 4 // STEPS
    v = v.reshape(N_Y, 2, 4, ROWS, width)
    near = [x.reshape(-1, 4, ROWS, width) for x in near]
    total = th.shape[0]
    t_spec = pl.BlockSpec((total, depth * width), lambda k, m: (0, k))
    return pl.pallas_call(
        sums_kernel,
        out_shape=jax.ShapeDtypeStruct((total, OUTER), jnp.float32),
        grid_spec=pltpu.PrefetchScalarGridSpec(
            num_scalar_prefetch=1,
            grid=(STEPS,),
            in_specs=[pl.BlockSpec((N_Y, 2, depth, ROWS, width), lambda k, m: (0, 0, k, 0, 0))]
            + [pl.BlockSpec((x.shape[0], depth, ROWS, width), lambda k, m: (0, k, 0, 0)) for x in near]
            + [t_spec, t_spec],
            out_specs=pl.BlockSpec((total, OUTER), lambda k, m: (0, 0)),
            scratch_shapes=[pltpu.VMEM((OUTER, depth * width), jnp.bfloat16)] * 2,
        ),
        compiler_params=pltpu.CompilerParams(vmem_limit_bytes=60 << 20),
        cost_estimate=pl.CostEstimate(flops=6 * th.size * OUTER, bytes_accessed=8 << 20, transcendentals=0),
    )(ys, v, *near, th, tl)


def along_y(x, by):
    return lax.ppermute(x, "y", [(i, (i + by) % N_Y) for i in range(N_Y)])


def gather_by_steps(own):
    down2, up2 = along_y(own, 2), along_y(own, -2)
    down1, up1 = along_y(own, 1), along_y(own, -1)
    down3, up3 = along_y(down2, 1), along_y(up2, -1)
    half = N_GROUP // 2
    down4, up4 = along_y(down2[:half], 2), along_y(up2[half:], -2)
    return [own, down1, up1, down2, up2, down3, up3, down4, up4]


def body(amplitudes, integrals, residual_in, cd_count):
    width = amplitudes.shape[2]
    live = cd_count[lax.axis_index(GROUP)] - lax.axis_index("zq") * (4 * width)

    both = jnp.broadcast_to(integrals[None], (2,) + integrals.shape).reshape(2 * N_GROUP, ROWS, width)
    v = lax.all_to_all(both, ("xh",) + GROUP, 0, 0, tiled=True)
    t = lax.all_to_all(amplitudes, GROUP, 0, 0, tiled=True)
    near = gather_by_steps(v[N_GROUP:])
    v = lax.all_gather(v[:N_GROUP], "y", axis=0)
    th, tl = pairs(live[None].astype(jnp.int32), t)

    offsets = jnp.array([near_y for near_y, _ in NEAR], jnp.int32)
    ys = (lax.axis_index("y").astype(jnp.int32) + N_Y + offsets) % N_Y
    sums = partial_sums(ys, v, near, th, tl)
    parts = lax.all_to_all(sums.reshape(N_ZQ * N_GROUP, ROWS, OUTER), ("zq",) + GROUP, 0, 0, tiled=True)
    return residual_in + jnp.sum(parts.reshape(N_ZQ, N_GROUP, ROWS, OUTER), axis=0)


def solution(mesh):
    mesh = Mesh(mesh.devices.reshape(2, 8, 2, 4, 2, 2), ("xh", "y", "core", "zq", "z0", "xl"))
    row, col = ("xh", "y", "core"), ("zq", "z0", "xl")
    in_specs = (P(None, row, col), P(None, row, col), P(None, row + col, None), P())
    return jax.shard_map(body, mesh=mesh, in_specs=in_specs, out_specs=P(None, row + col, None), check_vma=False)
```

```python
import functools

import jax
import jax.numpy as jnp
from jax import lax
from jax.experimental import pallas as pl
from jax.experimental.pallas import tpu as pltpu
from jax.sharding import Mesh, PartitionSpec as P

GROUP = ("xh", "z0", "xl")
N_Y, N_ZQ, N_GROUP = 8, 4, 8
ROWS = 16
OUTER = 512
HALF = OUTER // 2
STEPS = 2
VMEM_MB = 24

DOT = functools.partial(
    lax.dot_general, dimension_numbers=(((1,), (1,)), ((), ())), preferred_element_type=jnp.float32
)


def split(x):
    high = x.astype(jnp.bfloat16)
    return high, (x - high.astype(jnp.float32)).astype(jnp.bfloat16)


def pair_kernel(live, t_ref, th, tl):
    rows, width = t_ref.shape[1:]
    slots = lax.broadcasted_iota(jnp.int32, (rows, width), 1)
    for g in range(N_GROUP):
        xh, c = divmod(g, 4)
        at = (slice(xh * rows, (xh + 1) * rows), slice(c * width, (c + 1) * width))
        th[at], tl[at] = split(jnp.where(slots + c * width < live[0], t_ref[g], 0.0))


def pairs(live, t):
    rows, width = t.shape[1] // N_ZQ, t.shape[2]
    total = 2 * t.shape[1]
    return pl.pallas_call(
        pair_kernel,
        out_shape=[jax.ShapeDtypeStruct((total, 4 * width), jnp.bfloat16)] * 2,
        grid_spec=pltpu.PrefetchScalarGridSpec(
            num_scalar_prefetch=1,
            grid=(N_ZQ,),
            in_specs=[pl.BlockSpec((N_GROUP, rows, width), lambda zq, m: (0, zq, 0))],
            out_specs=[pl.BlockSpec((2 * rows, 4 * width), lambda zq, m: (zq, 0))] * 2,
        ),
        compiler_params=pltpu.CompilerParams(vmem_limit_bytes=16 << 20),
        cost_estimate=pl.CostEstimate(flops=3 * t.size, bytes_accessed=8 * t.size, transcendentals=0),
    )(live, t)


NEAR = (0, -1, 1, -2, 2, -3, 3, 4)


def sums_kernel(place, v_mine, v_other, th, tl, out, vh, vl):
    depth, width = v_mine.shape[2], v_mine.shape[4]
    for v_ref, core in ((v_mine, place[N_Y]), (v_other, 1 - place[N_Y])):
        for i in range(N_Y):
            for xh in range(2):
                start = pl.multiple_of(xh * HALF + place[i] * (2 * ROWS) + core * ROWS, ROWS)
                rows = pl.ds(start, ROWS)
                for c in range(depth):
                    columns = slice(c * width, (c + 1) * width)
                    vh[rows, columns], vl[rows, columns] = split(v_ref[i, xh, c])
    sums = DOT(th[...], vh[...]) + (DOT(tl[...], vh[...]) + DOT(th[...], vl[...]))

    @pl.when(pl.program_id(0) == 0)
    def _():
        out[...] = sums

    @pl.when(pl.program_id(0) > 0)
    def _():
        out[...] += sums


def partial_sums(place, mine, other, th, tl):
    width = mine.shape[2]
    depth = 4 // STEPS
    mine, other = (x.reshape(N_Y, 2, 4, ROWS, width) for x in (mine, other))
    total = th.shape[0]
    t_spec = pl.BlockSpec((total, depth * width), lambda k, m: (0, k))
    v_spec = pl.BlockSpec((N_Y, 2, depth, ROWS, width), lambda k, m: (0, 0, k, 0, 0))
    return pl.pallas_call(
        sums_kernel,
        out_shape=jax.ShapeDtypeStruct((total, OUTER), jnp.float32),
        grid_spec=pltpu.PrefetchScalarGridSpec(
            num_scalar_prefetch=1,
            grid=(STEPS,),
            in_specs=[v_spec, v_spec, t_spec, t_spec],
            out_specs=pl.BlockSpec((total, OUTER), lambda k, m: (0, 0)),
            scratch_shapes=[pltpu.VMEM((OUTER, depth * width), jnp.bfloat16)] * 2,
        ),
        compiler_params=pltpu.CompilerParams(vmem_limit_bytes=VMEM_MB << 20),
        cost_estimate=pl.CostEstimate(flops=6 * th.size * OUTER, bytes_accessed=8 << 20, transcendentals=0),
    )(place, mine, other, th, tl)


def along_y(x, by):
    return lax.ppermute(x, "y", [(i, (i + by) % N_Y) for i in range(N_Y)])


def gather(own):
    down2, up2 = along_y(own, 2), along_y(own, -2)
    down1, up1 = along_y(own, 1), along_y(own, -1)
    far = along_y(down2, 2)
    down3, up3 = along_y(down2, 1), along_y(up2, -1)
    return jnp.concatenate([own, down1, up1, down2, up2, down3, up3, far])


def body(amplitudes, integrals, residual_in, cd_count):
    width = amplitudes.shape[2]
    live = cd_count[lax.axis_index(GROUP)] - lax.axis_index("zq") * (4 * width)
    ys = (lax.axis_index("y").astype(jnp.int32) + N_Y + jnp.array(NEAR, jnp.int32)) % N_Y
    place = jnp.concatenate([ys, lax.axis_index("core").astype(jnp.int32)[None]])

    v = lax.all_to_all(integrals, GROUP, 0, 0, tiled=True)
    t = lax.all_to_all(amplitudes, GROUP, 0, 0, tiled=True)
    mine = gather(v)
    other = lax.ppermute(mine, "core", [(0, 1), (1, 0)])
    th, tl = pairs(live[None].astype(jnp.int32), t)

    sums = partial_sums(place, mine, other, th, tl)
    parts = lax.all_to_all(sums.reshape(N_ZQ * N_GROUP, ROWS, OUTER), ("zq",) + GROUP, 0, 0, tiled=True)
    return residual_in + jnp.sum(parts.reshape(N_ZQ, N_GROUP, ROWS, OUTER), axis=0)


def solution(mesh):
    mesh = Mesh(mesh.devices.reshape(2, 8, 2, 4, 2, 2), ("xh", "y", "core", "zq", "z0", "xl"))
    row, col = ("xh", "y", "core"), ("zq", "z0", "xl")
    in_specs = (P(None, row, col), P(None, row, col), P(None, row + col, None), P())
    return jax.shard_map(body, mesh=mesh, in_specs=in_specs, out_specs=P(None, row + col, None), check_vma=False)
```

```python
import functools

import jax
import jax.numpy as jnp
from jax import lax
from jax.experimental import pallas as pl
from jax.experimental.pallas import tpu as pltpu
from jax.sharding import Mesh, PartitionSpec as P

GROUP = ("xh", "z0", "xl")
N_Y, N_ZQ, N_GROUP = 8, 4, 8
ROWS = 16
OUTER = 512
HALF = OUTER // 2
STEPS = 2

DOT = functools.partial(
    lax.dot_general, dimension_numbers=(((1,), (1,)), ((), ())), preferred_element_type=jnp.float32
)


def split(x):
    high = x.astype(jnp.bfloat16)
    return high, (x - high.astype(jnp.float32)).astype(jnp.bfloat16)


NEAR = (0, -1, 1, -2, 2, -3, 3, 4)


def order_kernel(place, v_mine, v_other, vh, vl):
    width = v_mine.shape[4]
    for v_ref, core in ((v_mine, place[N_Y]), (v_other, 1 - place[N_Y])):
        for i in range(N_Y):
            for xh in range(2):
                start = pl.multiple_of(xh * HALF + place[i] * (2 * ROWS) + core * ROWS, ROWS)
                rows = pl.ds(start, ROWS)
                for c in range(4):
                    columns = slice(c * width, (c + 1) * width)
                    vh[rows, columns], vl[rows, columns] = split(v_ref[i, xh, c])


def in_order(place, mine, other):
    width = mine.shape[2]
    mine, other = (x.reshape(N_Y, 2, 4, ROWS, width) for x in (mine, other))
    v_spec = pl.BlockSpec(mine.shape, lambda k, m: (0, 0, 0, 0, 0))
    return pl.pallas_call(
        order_kernel,
        out_shape=[pltpu.HBM((OUTER, 4 * width), jnp.bfloat16)] * 2,
        grid_spec=pltpu.PrefetchScalarGridSpec(
            num_scalar_prefetch=1,
            grid=(1,),
            in_specs=[v_spec, v_spec],
            out_specs=[pl.BlockSpec((OUTER, 4 * width), lambda k, m: (0, 0))] * 2,
        ),
        compiler_params=pltpu.CompilerParams(vmem_limit_bytes=24 << 20),
        cost_estimate=pl.CostEstimate(flops=6 * mine.size, bytes_accessed=16 * mine.size, transcendentals=0),
    )(place, mine, other)


def sums_kernel(live, t_ref, vh, vl, out, th, tl):
    depth, rows, width = t_ref.shape[1:]
    rows = rows // N_ZQ
    slots = lax.broadcasted_iota(jnp.int32, (rows, width), 1) + pl.program_id(0) * (depth * width)
    for c in range(depth):
        alive = slots + c * width < live[0]
        for zq in range(N_ZQ):
            for xh in range(2):
                at = (slice((2 * zq + xh) * rows, (2 * zq + xh + 1) * rows), slice(c * width, (c + 1) * width))
                th[at], tl[at] = split(jnp.where(alive, t_ref[xh, c, zq * rows : (zq + 1) * rows], 0.0))
    sums = DOT(th[...], vh[...]) + (DOT(tl[...], vh[...]) + DOT(th[...], vl[...]))

    @pl.when(pl.program_id(0) == 0)
    def _():
        out[...] = sums

    @pl.when(pl.program_id(0) > 0)
    def _():
        out[...] += sums


def partial_sums(live, t, vh, vl):
    rows, width = t.shape[1:]
    depth = 4 // STEPS
    t = t.reshape(2, 4, rows, width)
    v_spec = pl.BlockSpec((OUTER, depth * width), lambda k, m: (0, k))
    return pl.pallas_call(
        sums_kernel,
        out_shape=jax.ShapeDtypeStruct((2 * rows, OUTER), jnp.float32),
        grid_spec=pltpu.PrefetchScalarGridSpec(
            num_scalar_prefetch=1,
            grid=(STEPS,),
            in_specs=[pl.BlockSpec((2, depth, rows, width), lambda k, m: (0, k, 0, 0)), v_spec, v_spec],
            out_specs=pl.BlockSpec((2 * rows, OUTER), lambda k, m: (0, 0)),
            scratch_shapes=[pltpu.VMEM((2 * rows, depth * width), jnp.bfloat16)] * 2,
        ),
        compiler_params=pltpu.CompilerParams(vmem_limit_bytes=24 << 20),
        cost_estimate=pl.CostEstimate(flops=6 * t.size * OUTER, bytes_accessed=8 << 20, transcendentals=0),
    )(live, t, vh, vl)


def along_y(x, by):
    return lax.ppermute(x, "y", [(i, (i + by) % N_Y) for i in range(N_Y)])


def gather(own):
    down2, up2 = along_y(own, 2), along_y(own, -2)
    down1, up1 = along_y(own, 1), along_y(own, -1)
    far = along_y(down2, 2)
    down3, up3 = along_y(down2, 1), along_y(up2, -1)
    return jnp.concatenate([own, down1, up1, down2, up2, down3, up3, far])


def body(amplitudes, integrals, residual_in, cd_count):
    width = amplitudes.shape[2]
    live = cd_count[lax.axis_index(GROUP)] - lax.axis_index("zq") * (4 * width)
    ys = (lax.axis_index("y").astype(jnp.int32) + N_Y + jnp.array(NEAR, jnp.int32)) % N_Y
    place = jnp.concatenate([ys, lax.axis_index("core").astype(jnp.int32)[None]])

    v = lax.all_to_all(integrals, GROUP, 0, 0, tiled=True)
    t = lax.all_to_all(amplitudes, GROUP, 0, 0, tiled=True)
    mine = gather(v)
    other = lax.ppermute(mine, "core", [(0, 1), (1, 0)])
    vh, vl = in_order(place, mine, other)

    sums = partial_sums(live[None].astype(jnp.int32), t, vh, vl)
    parts = lax.all_to_all(sums.reshape(N_ZQ * N_GROUP, ROWS, OUTER), ("zq",) + GROUP, 0, 0, tiled=True)
    return residual_in + jnp.sum(parts.reshape(N_ZQ, N_GROUP, ROWS, OUTER), axis=0)


def solution(mesh):
    mesh = Mesh(mesh.devices.reshape(2, 8, 2, 4, 2, 2), ("xh", "y", "core", "zq", "z0", "xl"))
    row, col = ("xh", "y", "core"), ("zq", "z0", "xl")
    in_specs = (P(None, row, col), P(None, row, col), P(None, row + col, None), P())
    return jax.shard_map(body, mesh=mesh, in_specs=in_specs, out_specs=P(None, row + col, None), check_vma=False)
```

```python
import functools

import jax
import jax.numpy as jnp
from jax import lax
from jax.experimental import pallas as pl
from jax.experimental.pallas import tpu as pltpu
from jax.sharding import Mesh, PartitionSpec as P

GROUP = ("xh", "z0", "xl")
N_Y, N_ZQ, N_GROUP = 8, 4, 8
ROWS = 16
OUTER = 512
HALF = OUTER // 2
STEPS = 2

DOT = functools.partial(
    lax.dot_general, dimension_numbers=(((1,), (1,)), ((), ())), preferred_element_type=jnp.float32
)


def split(x):
    high = x.astype(jnp.bfloat16)
    return high, (x - high.astype(jnp.float32)).astype(jnp.bfloat16)


NEAR = (0, -1, 1, -2, 2, -3, 3, 4)


def sums_kernel(place, t_ref, v_mine, v_other, out, th, tl, vh, vl):
    depth, rows, width = t_ref.shape[1:]
    rows = rows // N_ZQ
    slots = lax.broadcasted_iota(jnp.int32, (rows, width), 1) + pl.program_id(0) * (depth * width)
    for c in range(depth):
        columns = slice(c * width, (c + 1) * width)
        alive = slots + c * width < place[N_Y + 1]
        for zq in range(N_ZQ):
            for xh in range(2):
                at = (slice((2 * zq + xh) * rows, (2 * zq + xh + 1) * rows), columns)
                th[at], tl[at] = split(jnp.where(alive, t_ref[xh, c, zq * rows : (zq + 1) * rows], 0.0))
    for v_ref, core in ((v_mine, place[N_Y]), (v_other, 1 - place[N_Y])):
        for i in range(N_Y):
            for xh in range(2):
                start = pl.multiple_of(xh * HALF + place[i] * (2 * ROWS) + core * ROWS, ROWS)
                for c in range(depth):
                    at = (pl.ds(start, ROWS), slice(c * width, (c + 1) * width))
                    vh[at], vl[at] = split(v_ref[i, xh, c])
    sums = DOT(th[...], vh[...]) + (DOT(tl[...], vh[...]) + DOT(th[...], vl[...]))

    @pl.when(pl.program_id(0) == 0)
    def _():
        out[...] = sums

    @pl.when(pl.program_id(0) > 0)
    def _():
        out[...] += sums


def partial_sums(place, t, mine, other):
    rows, width = t.shape[1:]
    depth = 4 // STEPS
    t = t.reshape(2, 4, rows, width)
    mine, other = (x.reshape(N_Y, 2, 4, ROWS, width) for x in (mine, other))
    v_spec = pl.BlockSpec((N_Y, 2, depth, ROWS, width), lambda k, m: (0, 0, k, 0, 0))
    return pl.pallas_call(
        sums_kernel,
        out_shape=jax.ShapeDtypeStruct((2 * rows, OUTER), jnp.float32),
        grid_spec=pltpu.PrefetchScalarGridSpec(
            num_scalar_prefetch=1,
            grid=(STEPS,),
            in_specs=[pl.BlockSpec((2, depth, rows, width), lambda k, m: (0, k, 0, 0)), v_spec, v_spec],
            out_specs=pl.BlockSpec((2 * rows, OUTER), lambda k, m: (0, 0)),
            scratch_shapes=[pltpu.VMEM((2 * rows, depth * width), jnp.bfloat16)] * 2
            + [pltpu.VMEM((OUTER, depth * width), jnp.bfloat16)] * 2,
        ),
        compiler_params=pltpu.CompilerParams(vmem_limit_bytes=24 << 20),
        cost_estimate=pl.CostEstimate(flops=6 * t.size * OUTER, bytes_accessed=8 << 20, transcendentals=0),
    )(place, t, mine, other)


def along_y(x, by):
    return lax.ppermute(x, "y", [(i, (i + by) % N_Y) for i in range(N_Y)])


def gather(own):
    down2, up2 = along_y(own, 2), along_y(own, -2)
    down1, up1 = along_y(own, 1), along_y(own, -1)
    far = along_y(down2, 2)
    down3, up3 = along_y(down2, 1), along_y(up2, -1)
    return jnp.concatenate([own, down1, up1, down2, up2, down3, up3, far])


def body(amplitudes, integrals, residual_in, cd_count):
    width = amplitudes.shape[2]
    live = cd_count[lax.axis_index(GROUP)] - lax.axis_index("zq") * (4 * width)
    ys = (lax.axis_index("y").astype(jnp.int32) + N_Y + jnp.array(NEAR, jnp.int32)) % N_Y
    place = jnp.concatenate([ys, jnp.stack([lax.axis_index("core"), live]).astype(jnp.int32)])

    v = lax.all_to_all(integrals, GROUP, 0, 0, tiled=True)
    t = lax.all_to_all(amplitudes, GROUP, 0, 0, tiled=True)
    mine = gather(v)
    other = lax.ppermute(mine, "core", [(0, 1), (1, 0)])

    sums = partial_sums(place, t, mine, other)
    parts = lax.all_to_all(sums.reshape(N_ZQ * N_GROUP, ROWS, OUTER), ("zq",) + GROUP, 0, 0, tiled=True)
    return residual_in + jnp.sum(parts.reshape(N_ZQ, N_GROUP, ROWS, OUTER), axis=0)


def solution(mesh):
    mesh = Mesh(mesh.devices.reshape(2, 8, 2, 4, 2, 2), ("xh", "y", "core", "zq", "z0", "xl"))
    row, col = ("xh", "y", "core"), ("zq", "z0", "xl")
    in_specs = (P(None, row, col), P(None, row, col), P(None, row + col, None), P())
    return jax.shard_map(body, mesh=mesh, in_specs=in_specs, out_specs=P(None, row + col, None), check_vma=False)
```

```python
import functools

import jax
import jax.numpy as jnp
from jax import lax
from jax.experimental import pallas as pl
from jax.experimental.pallas import tpu as pltpu
from jax.sharding import Mesh, PartitionSpec as P

GROUP = ("xh", "z0", "xl")
N_Y, N_ZQ, N_GROUP = 8, 4, 8
ROWS = 16
OUTER = 512
HALF = OUTER // 2

DOT = functools.partial(
    lax.dot_general, dimension_numbers=(((1,), (1,)), ((), ())), preferred_element_type=jnp.float32
)


def split(x):
    high = x.astype(jnp.bfloat16)
    return high, (x - high.astype(jnp.float32)).astype(jnp.bfloat16)


NEAR = (0, -1, 1, -2, 2, -3, 3, 4)


def put(ref, rows, c, halves, which):
    width = halves[0].shape[1]
    depth = ref.shape[1] // (3 * width)
    for i, half in enumerate(which):
        start = (i * depth + c) * width
        ref[rows, start : start + width] = halves[half]


def sums_kernel(place, t_ref, mine_ref, other_ref, out, ts, vs, v_mine, v_other, sems):
    copies = [
        pltpu.make_async_copy(source, held, sems.at[i])
        for i, (source, held) in enumerate(((mine_ref, v_mine), (other_ref, v_other)))
    ]
    for copy in copies:
        copy.start()
    depth, rows, width = t_ref.shape[1:]
    rows = rows // N_ZQ
    slots = lax.broadcasted_iota(jnp.int32, (rows, width), 1)
    for c in range(depth):
        columns = slice(c * width, (c + 1) * width)
        alive = slots + c * width < place[N_Y + 1]
        for zq in range(N_ZQ):
            for xh in range(2):
                at = (slice((2 * zq + xh) * rows, (2 * zq + xh + 1) * rows), columns)
                put(ts, at[0], c, split(jnp.where(alive, t_ref[xh, c, zq * rows : (zq + 1) * rows], 0.0)), (0, 1, 0))
    for copy, v_ref, core in zip(copies, (v_mine, v_other), (place[N_Y], 1 - place[N_Y])):
        copy.wait()
        for i in range(N_Y):
            for xh in range(2):
                start = pl.multiple_of(xh * HALF + place[i] * (2 * ROWS) + core * ROWS, ROWS)
                for c in range(depth):
                    put(vs, pl.ds(start, ROWS), c, split(v_ref[i, xh, c]), (0, 0, 1))
    out[...] = DOT(ts[...], vs[...])


def partial_sums(place, t, mine, other):
    rows, width = t.shape[1:]
    t = t.reshape(2, 4, rows, width)
    mine, other = (x.reshape(N_Y, 2, 4, ROWS, width) for x in (mine, other))
    deep = 12 * width
    held = pltpu.VMEM(mine.shape, mine.dtype)
    return pl.pallas_call(
        sums_kernel,
        out_shape=jax.ShapeDtypeStruct((2 * rows, OUTER), jnp.float32),
        grid_spec=pltpu.PrefetchScalarGridSpec(
            num_scalar_prefetch=1,
            grid=(1,),
            in_specs=[pl.BlockSpec(t.shape, lambda k, m: (0, 0, 0, 0))] + [pl.BlockSpec(memory_space=pl.ANY)] * 2,
            out_specs=pl.BlockSpec((2 * rows, OUTER), lambda k, m: (0, 0)),
            scratch_shapes=[
                pltpu.VMEM((2 * rows, deep), jnp.bfloat16),
                pltpu.VMEM((OUTER, deep), jnp.bfloat16),
                held,
                held,
                pltpu.SemaphoreType.DMA((2,)),
            ],
        ),
        compiler_params=pltpu.CompilerParams(vmem_limit_bytes=32 << 20),
        cost_estimate=pl.CostEstimate(flops=6 * t.size * OUTER, bytes_accessed=8 << 20, transcendentals=0),
    )(place, t, mine, other)


def along_y(x, by):
    return lax.ppermute(x, "y", [(i, (i + by) % N_Y) for i in range(N_Y)])


def gather(own):
    down2, up2 = along_y(own, 2), along_y(own, -2)
    down1, up1 = along_y(own, 1), along_y(own, -1)
    far = along_y(down2, 2)
    down3, up3 = along_y(down2, 1), along_y(up2, -1)
    return jnp.concatenate([own, down1, up1, down2, up2, down3, up3, far])


def body(amplitudes, integrals, residual_in, cd_count):
    width = amplitudes.shape[2]
    live = cd_count[lax.axis_index(GROUP)] - lax.axis_index("zq") * (4 * width)
    ys = (lax.axis_index("y").astype(jnp.int32) + N_Y + jnp.array(NEAR, jnp.int32)) % N_Y
    place = jnp.concatenate([ys, jnp.stack([lax.axis_index("core"), live]).astype(jnp.int32)])

    v = lax.all_to_all(integrals, GROUP, 0, 0, tiled=True)
    t = lax.all_to_all(amplitudes, GROUP, 0, 0, tiled=True)
    mine = gather(v)
    other = lax.ppermute(mine, "core", [(0, 1), (1, 0)])

    sums = partial_sums(place, t, mine, other)
    parts = lax.all_to_all(sums.reshape(N_ZQ * N_GROUP, ROWS, OUTER), ("zq",) + GROUP, 0, 0, tiled=True)
    return residual_in + jnp.sum(parts.reshape(N_ZQ, N_GROUP, ROWS, OUTER), axis=0)


def solution(mesh):
    mesh = Mesh(mesh.devices.reshape(2, 8, 2, 4, 2, 2), ("xh", "y", "core", "zq", "z0", "xl"))
    row, col = ("xh", "y", "core"), ("zq", "z0", "xl")
    in_specs = (P(None, row, col), P(None, row, col), P(None, row + col, None), P())
    return jax.shard_map(body, mesh=mesh, in_specs=in_specs, out_specs=P(None, row + col, None), check_vma=False)
```

```python
import functools

import jax
import jax.numpy as jnp
from jax import lax
from jax.experimental import pallas as pl
from jax.experimental.pallas import tpu as pltpu
from jax.sharding import Mesh, PartitionSpec as P

GROUP = ("xh", "z0", "xl")
N_Y, N_ZQ, N_GROUP = 8, 4, 8
ROWS = 16
OUTER = 512
HALF = OUTER // 2

DOT = functools.partial(
    lax.dot_general, dimension_numbers=(((1,), (1,)), ((), ())), preferred_element_type=jnp.float32
)


def split(x):
    high = x.astype(jnp.bfloat16)
    return high, (x - high.astype(jnp.float32)).astype(jnp.bfloat16)


NEAR = (0, -1, 1, -2, 2, -3, 3, 4)


def put(ref, rows, c, halves, which):
    width = halves[0].shape[1]
    depth = ref.shape[1] // (3 * width)
    for i, half in enumerate(which):
        start = (i * depth + c) * width
        ref[rows, start : start + width] = halves[half]


def sums_kernel(place, t_ref, mine_ref, other_ref, out, ts, vs, v_mine, v_other, sems):
    copies = [
        pltpu.make_async_copy(source, held, sems.at[i])
        for i, (source, held) in enumerate(((mine_ref, v_mine), (other_ref, v_other)))
    ]
    for copy in copies:
        copy.start()
    depth, rows, width = t_ref.shape[1:]
    rows = rows // N_ZQ
    slots = lax.broadcasted_iota(jnp.int32, (rows, width), 1)
    for c in range(depth):
        columns = slice(c * width, (c + 1) * width)
        alive = slots + c * width < place[N_Y + 1]
        for zq in range(N_ZQ):
            for xh in range(2):
                at = (slice((2 * zq + xh) * rows, (2 * zq + xh + 1) * rows), columns)
                put(ts, at[0], c, split(jnp.where(alive, t_ref[xh, c, zq * rows : (zq + 1) * rows], 0.0)), (0, 1, 0))
    for copy, v_ref, core in zip(copies, (v_mine, v_other), (place[N_Y], 1 - place[N_Y])):
        copy.wait()
        for i in range(N_Y):
            for xh in range(2):
                start = pl.multiple_of(xh * HALF + place[i] * (2 * ROWS) + core * ROWS, ROWS)
                for c in range(depth):
                    put(vs, pl.ds(start, ROWS), c, split(v_ref[i, xh, c]), (0, 0, 1))
    out[...] = DOT(ts[...], vs[...])


def partial_sums(place, t, mine, other):
    rows, width = t.shape[1:]
    t = t.reshape(2, 4, rows, width)
    mine, other = (x.reshape(N_Y, 2, 4, ROWS, width) for x in (mine, other))
    deep = 12 * width
    held = pltpu.VMEM(mine.shape, mine.dtype)
    return pl.pallas_call(
        sums_kernel,
        out_shape=jax.ShapeDtypeStruct((2 * rows, OUTER), jnp.float32),
        grid_spec=pltpu.PrefetchScalarGridSpec(
            num_scalar_prefetch=1,
            grid=(),
            in_specs=[pl.BlockSpec(memory_space=pltpu.VMEM)] + [pl.BlockSpec(memory_space=pl.ANY)] * 2,
            out_specs=pl.BlockSpec(memory_space=pltpu.VMEM),
            scratch_shapes=[
                pltpu.VMEM((2 * rows, deep), jnp.bfloat16),
                pltpu.VMEM((OUTER, deep), jnp.bfloat16),
                held,
                held,
                pltpu.SemaphoreType.DMA((2,)),
            ],
        ),
        compiler_params=pltpu.CompilerParams(vmem_limit_bytes=32 << 20),
        cost_estimate=pl.CostEstimate(flops=6 * t.size * OUTER, bytes_accessed=8 << 20, transcendentals=0),
    )(place, t, mine, other)


def along_y(x, by):
    return lax.ppermute(x, "y", [(i, (i + by) % N_Y) for i in range(N_Y)])


def gather(own):
    down2, up2 = along_y(own, 2), along_y(own, -2)
    down1, up1 = along_y(own, 1), along_y(own, -1)
    far = along_y(down2, 2)
    down3, up3 = along_y(down2, 1), along_y(up2, -1)
    return jnp.concatenate([own, down1, up1, down2, up2, down3, up3, far])


def body(amplitudes, integrals, residual_in, cd_count):
    width = amplitudes.shape[2]
    live = cd_count[lax.axis_index(GROUP)] - lax.axis_index("zq") * (4 * width)
    ys = (lax.axis_index("y").astype(jnp.int32) + N_Y + jnp.array(NEAR, jnp.int32)) % N_Y
    place = jnp.concatenate([ys, jnp.stack([lax.axis_index("core"), live]).astype(jnp.int32)])

    v = lax.all_to_all(integrals, GROUP, 0, 0, tiled=True)
    t = lax.all_to_all(amplitudes, GROUP, 0, 0, tiled=True)
    mine = gather(v)
    other = lax.ppermute(mine, "core", [(0, 1), (1, 0)])

    sums = partial_sums(place, t, mine, other)
    parts = lax.all_to_all(sums.reshape(N_ZQ * N_GROUP, ROWS, OUTER), ("zq",) + GROUP, 0, 0, tiled=True)
    return residual_in + jnp.sum(parts.reshape(N_ZQ, N_GROUP, ROWS, OUTER), axis=0)


def solution(mesh):
    mesh = Mesh(mesh.devices.reshape(2, 8, 2, 4, 2, 2), ("xh", "y", "core", "zq", "z0", "xl"))
    row, col = ("xh", "y", "core"), ("zq", "z0", "xl")
    in_specs = (P(None, row, col), P(None, row, col), P(None, row + col, None), P())
    return jax.shard_map(body, mesh=mesh, in_specs=in_specs, out_specs=P(None, row + col, None), check_vma=False)
```

```python
import functools

import jax
import jax.numpy as jnp
from jax import lax
from jax.experimental import pallas as pl
from jax.experimental.pallas import tpu as pltpu
from jax.sharding import Mesh, PartitionSpec as P

GROUP = ("xh", "z0", "xl")
N_Y, N_ZQ, N_GROUP = 8, 4, 8
ROWS = 16
OUTER = 512
HALF = OUTER // 2

DOT = functools.partial(
    lax.dot_general, dimension_numbers=(((1,), (1,)), ((), ())), preferred_element_type=jnp.float32
)


def split(x):
    high = x.astype(jnp.bfloat16)
    return high, (x - high.astype(jnp.float32)).astype(jnp.bfloat16)


NEAR = (0, -1, 1, -2, 2, -3, 3, 4)


def put(ref, rows, c, halves, which):
    width = halves[0].shape[1]
    depth = ref.shape[1] // (3 * width)
    for i, half in enumerate(which):
        start = (i * depth + c) * width
        ref[rows, start : start + width] = halves[half]


def sums_kernel(place, t_ref, mine_ref, other_ref, out, ts, ts_late, vs, v_mine, v_other, sems):
    copies = [
        pltpu.make_async_copy(source, held, sems.at[i])
        for i, (source, held) in enumerate(((mine_ref, v_mine), (other_ref, v_other)))
    ]
    for copy in copies:
        copy.start()
    depth, rows, width = t_ref.shape[1:]
    rows = rows // N_ZQ
    slots = lax.broadcasted_iota(jnp.int32, (rows, width), 1)

    def fill(ref, first):
        for c in range(depth):
            alive = slots + c * width < place[N_Y + 1]
            for i in range(N_ZQ // 2):
                for xh in range(2):
                    block = t_ref[xh, c, (first + i) * rows : (first + i + 1) * rows]
                    at = slice((2 * i + xh) * rows, (2 * i + xh + 1) * rows)
                    put(ref, at, c, split(jnp.where(alive, block, 0.0)), (0, 1, 0))

    fill(ts, 0)
    for copy, v_ref, core in zip(copies, (v_mine, v_other), (place[N_Y], 1 - place[N_Y])):
        copy.wait()
        for i in range(N_Y):
            for xh in range(2):
                start = pl.multiple_of(xh * HALF + place[i] * (2 * ROWS) + core * ROWS, ROWS)
                for c in range(depth):
                    put(vs, pl.ds(start, ROWS), c, split(v_ref[i, xh, c]), (0, 0, 1))
    half = out.shape[0] // 2
    out[:half] = DOT(ts[...], vs[...])
    fill(ts_late, N_ZQ // 2)
    out[half:] = DOT(ts_late[...], vs[...])


def partial_sums(place, t, mine, other):
    rows, width = t.shape[1:]
    t = t.reshape(2, 4, rows, width)
    mine, other = (x.reshape(N_Y, 2, 4, ROWS, width) for x in (mine, other))
    deep = 12 * width
    held = pltpu.VMEM(mine.shape, mine.dtype)
    return pl.pallas_call(
        sums_kernel,
        out_shape=jax.ShapeDtypeStruct((2 * rows, OUTER), jnp.float32),
        grid_spec=pltpu.PrefetchScalarGridSpec(
            num_scalar_prefetch=1,
            grid=(),
            in_specs=[pl.BlockSpec(memory_space=pltpu.VMEM)] + [pl.BlockSpec(memory_space=pl.ANY)] * 2,
            out_specs=pl.BlockSpec(memory_space=pltpu.VMEM),
            scratch_shapes=[
                pltpu.VMEM((rows, deep), jnp.bfloat16),
                pltpu.VMEM((rows, deep), jnp.bfloat16),
                pltpu.VMEM((OUTER, deep), jnp.bfloat16),
                held,
                held,
                pltpu.SemaphoreType.DMA((2,)),
            ],
        ),
        compiler_params=pltpu.CompilerParams(vmem_limit_bytes=32 << 20),
        cost_estimate=pl.CostEstimate(flops=6 * t.size * OUTER, bytes_accessed=8 << 20, transcendentals=0),
    )(place, t, mine, other)


def along_y(x, by):
    return lax.ppermute(x, "y", [(i, (i + by) % N_Y) for i in range(N_Y)])


def gather(own):
    down2, up2 = along_y(own, 2), along_y(own, -2)
    down1, up1 = along_y(own, 1), along_y(own, -1)
    far = along_y(down2, 2)
    down3, up3 = along_y(down2, 1), along_y(up2, -1)
    return jnp.concatenate([own, down1, up1, down2, up2, down3, up3, far])


def body(amplitudes, integrals, residual_in, cd_count):
    width = amplitudes.shape[2]
    live = cd_count[lax.axis_index(GROUP)] - lax.axis_index("zq") * (4 * width)
    ys = (lax.axis_index("y").astype(jnp.int32) + N_Y + jnp.array(NEAR, jnp.int32)) % N_Y
    place = jnp.concatenate([ys, jnp.stack([lax.axis_index("core"), live]).astype(jnp.int32)])

    v = lax.all_to_all(integrals, GROUP, 0, 0, tiled=True)
    t = lax.all_to_all(amplitudes, GROUP, 0, 0, tiled=True)
    mine = gather(v)
    other = lax.ppermute(mine, "core", [(0, 1), (1, 0)])

    sums = partial_sums(place, t, mine, other)
    parts = lax.all_to_all(sums.reshape(N_ZQ * N_GROUP, ROWS, OUTER), ("zq",) + GROUP, 0, 0, tiled=True)
    return residual_in + jnp.sum(parts.reshape(N_ZQ, N_GROUP, ROWS, OUTER), axis=0)


def solution(mesh):
    mesh = Mesh(mesh.devices.reshape(2, 8, 2, 4, 2, 2), ("xh", "y", "core", "zq", "z0", "xl"))
    row, col = ("xh", "y", "core"), ("zq", "z0", "xl")
    in_specs = (P(None, row, col), P(None, row, col), P(None, row + col, None), P())
    return jax.shard_map(body, mesh=mesh, in_specs=in_specs, out_specs=P(None, row + col, None), check_vma=False)
```
